512 devices in a mesh: blk: 128 (over x, z, y_lo), lane: 4 (over y_hi, core).
Axes of the slice: x: 4, y: 4 (y_hi: 2, y_lo: 2; y = y_hi * 2 + y_lo), z: 16, core: 2. Of those that a mesh axis runs over, the one named last changes fastest.
Arguments:
- left_factor: bfloat16 [65536, 512], P('blk'), may hold values from -6 to 6
- right_factor: bfloat16 [4, 65536, 512], P('lane', 'blk'), may hold values from -6 to 6
- observed: bfloat16 [4, 4, 512, 65536], P('lane', None, None, 'blk'), may hold values from -6 to 6
- row_codes: int32 [65536], P('blk'), may hold values from 0 to 1073741823
- shift_codes: int32 [4, 4, 65536], P('lane', None, 'blk'), may hold values from 0 to 29
Outputs:
- left_out: bfloat16 [65536, 512], P('blk')
- right_out: bfloat16 [4, 65536, 512], P('lane', 'blk')
The draws below stay inside these ranges and needn't reach their ends.
Inputs may be any that keep to these rules, and one draw needn't show every extreme that they name: `row_codes`: each row's word carries thirty independent sampling bits. `shift_codes`: A bit number for each lane, cycle step and visited tile entry column.
All inputs are finite; a program needn't handle non-finite values.
Results may differ from the reference program's by a relative error of at most 0.013.
Values may be sent and summed in bfloat16 or wider, within the bound.
No kernel may reach another device: no remote copies, remote signals or barrier semaphores. Data moves between devices by JAX's collectives and lax.ppermute only.
A program may use at most 64 MiB of HBM per device.

```python
import math
import jax
import jax.numpy as jnp
from jax import lax

RANK = 512
TILE_COLS = 512
TILE_ROWS = 512
STEPS = 4
BLOCKS = 128
ROWS = 65536
COLUMNS = 65536
N_LANE = 4


def touch_ends(drawn, rng, low, high):
    longest = drawn.shape.index(max(drawn.shape))
    spots = []
    for shift in (0, 1):
        where = [jax.random.randint(jax.random.fold_in(rng, axis), (), 0, length) for axis, length in enumerate(drawn.shape)]
        where[longest] = (where[longest] + shift) % drawn.shape[longest]
        spots.append(tuple(where))
    return drawn.at[spots[0]].set(low).at[spots[1]].set(high)


def steps_of(rng, shape, pieces, smallest, high):
    gain = 1.0
    for axis_at, shards_of in pieces:
        steps = jax.random.uniform(jax.random.fold_in(jax.random.fold_in(rng, 6), axis_at), (shards_of,), jnp.float32, smallest / len(pieces), high / len(pieces))
        gain = gain * jnp.repeat(jnp.exp(steps), shape[axis_at] // shards_of).reshape((-1,) + (1,) * (len(shape) - 1 - axis_at))
    return gain


def normal_values(rng, dims, scale, reach, split=(), kind=jnp.bfloat16):
    drawn = jax.random.normal(rng, dims, jnp.float32) * scale
    if len(split) > 0:
        drawn = steps_of(rng, dims, split, -0.22, 0.18) * drawn
    return jnp.clip(drawn, min=-reach, max=reach).astype(kind)


def setup_inputs(seed: int = 0) -> dict:
    key_list = jax.random.split(jax.random.key(seed), 6)
    left_factor = normal_values(key_list[0], (ROWS, RANK), 1.0, 6.0, ((0, 128),))
    right_factor = normal_values(key_list[1], (N_LANE, COLUMNS, RANK), 1.0, 6.0, ((0, 4), (1, 128)))
    observed = normal_values(key_list[2], (N_LANE, STEPS, TILE_COLS, ROWS), 1.0, 6.0, ((0, 4), (3, 128)))
    row_codes = touch_ends(jax.random.randint(key_list[3], (ROWS,), 0, 1073741824), jax.random.fold_in(key_list[3], 1), 0, 1073741823).astype(jnp.int32)
    shift_codes = touch_ends(jax.random.randint(key_list[4], (N_LANE, STEPS, COLUMNS), 0, 30), jax.random.fold_in(key_list[4], 1), 0, 29).astype(jnp.int32)
    return {"left_factor": left_factor, "right_factor": right_factor, "observed": observed, "row_codes": row_codes, "shift_codes": shift_codes}


step_right = 0.25
step_left = 0.1

def reference(left_factor, right_factor, observed, row_codes, shift_codes):
    root_scale = 1.0 / math.sqrt(RANK)
    left_blocks = left_factor.reshape(BLOCKS, TILE_ROWS, RANK).astype(jnp.float32)
    row_blocks = row_codes.reshape(BLOCKS, TILE_ROWS)
    grad_total = jnp.zeros((BLOCKS, TILE_ROWS, RANK), jnp.float32)
    right_list = []
    for lane_index in range(N_LANE):
        right_now = right_factor[lane_index].reshape(BLOCKS, TILE_COLS, RANK)
        for cycle_step in range(STEPS):
            visited = jnp.roll(right_now, cycle_step, axis=0).astype(jnp.float32)
            predicted = jnp.einsum('nck,nrk->ncr', visited, left_blocks) * root_scale
            shifts = shift_codes[lane_index, cycle_step].reshape(BLOCKS, TILE_COLS)
            sample_bits = jnp.right_shift(row_blocks[:, None, :], shifts[:, :, None]) & 1
            target = observed[lane_index, cycle_step].reshape(TILE_COLS, BLOCKS, TILE_ROWS)
            target = jnp.transpose(target, (1, 0, 2)).astype(jnp.float32)
            error_tile = jnp.where(sample_bits == 1, predicted - target, 0.0).astype(jnp.bfloat16)
            error_tile = lax.optimization_barrier(error_tile).astype(jnp.float32)
            grad_right = jnp.einsum('ncr,nrk->nck', error_tile, left_blocks)
            grad_total = grad_total + jnp.einsum('ncr,nck->nrk', error_tile, visited)
            updated = (visited - step_right * root_scale * grad_right).astype(jnp.bfloat16)
            right_now = jnp.roll(updated, -cycle_step, axis=0)
        placed = jnp.roll(right_now, STEPS - 1, axis=0)
        right_list.append(placed.reshape(BLOCKS * TILE_COLS, RANK))
    left_out = (left_blocks - step_left * root_scale * grad_total).astype(jnp.bfloat16)
    return (left_out.reshape(BLOCKS * TILE_ROWS, RANK), jnp.stack(right_list))
```

```python
import math

import jax
import jax.numpy as jnp
from jax import lax
from jax.sharding import PartitionSpec as P

step_right = 0.25
step_left = 0.1
chunk_rows = (128, 128, 128, 128)


def passed_along(value):
    count = lax.axis_size("blk")
    return lax.ppermute(value, "blk", [(i, (i + 1) % count) for i in range(count)])


def swapped(value, bit):
    count = lax.axis_size("lane")
    return lax.ppermute(value, "lane", [(i, i ^ bit) for i in range(count)])


def visit(right_part, left_factor, target, row_codes, shifts, root_scale):
    predicted = (
        lax.dot_general(
            right_part, left_factor, (((1,), (1,)), ((), ())), preferred_element_type=jnp.float32
        )
        * root_scale
    )
    sample_bits = jnp.right_shift(row_codes[None, :], shifts[:, None]) & 1
    error_tile = jnp.where(sample_bits == 1, predicted - target.astype(jnp.float32), 0.0).astype(
        jnp.bfloat16
    )
    grad_right = jnp.dot(error_tile, left_factor, preferred_element_type=jnp.float32)
    updated = (right_part.astype(jnp.float32) - step_right * root_scale * grad_right).astype(
        jnp.bfloat16
    )
    return updated, error_tile


def local(left_factor, right_factor, observed, row_codes, shift_codes):
    rank_size = left_factor.shape[1]
    root_scale = 1.0 / math.sqrt(rank_size)
    cycle_steps = observed.shape[1]
    firsts = [sum(chunk_rows[:i]) for i in range(len(chunk_rows))]
    parts = [right_factor[0, a : a + n] for a, n in zip(firsts, chunk_rows)]
    grad_sum = jnp.zeros(left_factor.shape, jnp.float32)
    for s in range(cycle_steps):
        for i, (a, n) in enumerate(zip(firsts, chunk_rows)):
            updated, error_tile = visit(
                parts[i],
                left_factor,
                observed[0, s, a : a + n],
                row_codes,
                shift_codes[0, s, a : a + n],
                root_scale,
            )
            grad_sum = grad_sum + lax.dot_general(
                error_tile, parts[i], (((0,), (0,)), ((), ())), preferred_element_type=jnp.float32
            )
            parts[i] = updated if s + 1 == cycle_steps else passed_along(updated)
    right_out = jnp.concatenate(parts, axis=0)[None]

    half = left_factor.shape[0] // 2
    core = lax.axis_index("lane") % 2
    theirs = lax.dynamic_slice_in_dim(grad_sum, (1 - core) * half, half, 0)
    mine = lax.dynamic_slice_in_dim(grad_sum, core * half, half, 0)
    own_rows = lax.dynamic_slice_in_dim(left_factor, core * half, half, 0)
    chip_sum = (mine + swapped(theirs.astype(jnp.bfloat16), 1).astype(jnp.float32)).astype(
        jnp.bfloat16
    )
    total = chip_sum.astype(jnp.float32) + swapped(chip_sum, 2).astype(jnp.float32)
    renewed = (own_rows.astype(jnp.float32) - step_left * root_scale * total).astype(jnp.bfloat16)
    other = swapped(renewed, 1)
    left_out = jnp.concatenate(
        [jnp.where(core == 0, renewed, other), jnp.where(core == 0, other, renewed)], axis=0
    )
    return left_out, right_out


def solution(mesh):
    in_specs = (
        P("blk", None),
        P("lane", "blk", None),
        P("lane", None, None, "blk"),
        P("blk"),
        P("lane", None, "blk"),
    )
    out_specs = (P("blk", None), P("lane", "blk", None))
    return jax.shard_map(local, mesh=mesh, in_specs=in_specs, out_specs=out_specs, check_vma=False)
```

```python
import functools
import math

import jax
import jax.numpy as jnp
from jax import lax
from jax.experimental import pallas as pl
from jax.experimental.pallas import tpu as pltpu
from jax.sharding import PartitionSpec as P

step_right = 0.25
step_left = 0.1
f32 = jnp.float32
bf16 = jnp.bfloat16
vmem_bytes = 12 << 20
in_vmem = pl.BlockSpec(memory_space=pltpu.VMEM)
in_hbm = pl.BlockSpec(memory_space=pltpu.HBM)
params = pltpu.CompilerParams(vmem_limit_bytes=vmem_bytes)


def passed_along(value):
    count = lax.axis_size("blk")
    return lax.ppermute(value, "blk", [(i, (i + 1) % count) for i in range(count)])


def both(value, bit):
    groups = [[i, i ^ bit] for i in range(lax.axis_size("lane")) if i < i ^ bit]
    return lax.all_gather(value, "lane", axis=0, axis_index_groups=groups, tiled=False)


def keep_hbm(*arrays):
    return [pltpu.with_memory_space_constraint(x, pltpu.HBM) for x in arrays]


def keep_vmem(*arrays):
    return [pltpu.with_memory_space_constraint(x, pltpu.VMEM) for x in arrays]


def cost(n, w, products):
    return pl.CostEstimate(flops=2 * products * n * w * w, bytes_accessed=8 * n * w, transcendentals=0)


def times_transposed(a, left):
    return lax.dot_general(a, left, (((1,), (1,)), ((), ())), preferred_element_type=f32)


def errors(predicted, target, codes, shifts, scale):
    rows, columns = predicted.shape
    by_row = jnp.broadcast_to(shifts, (128, rows)).T
    by_row = jnp.concatenate([by_row] * (columns // 128), axis=1)
    bits = jnp.right_shift(jnp.broadcast_to(codes, (rows, columns)), by_row) & 1
    return jnp.where(bits == 1, predicted * scale - target.astype(f32), 0.0).astype(bf16)


def stepped(right, error, left, scale):
    grad = jnp.dot(error, left, preferred_element_type=f32)
    return (right.astype(f32) - step_right * scale * grad).astype(bf16)


def first_kernel(n, scale, right_hbm, left_hbm, observed_hbm, codes_hbm, shifts_hbm,
                 out, error, right, left, codes, shifts, target, sems):
    pairs = [
        (right_hbm.at[0, pl.ds(0, n)], right),
        (left_hbm, left),
        (codes_hbm, codes),
        (shifts_hbm, shifts),
        (observed_hbm.at[0, 0, pl.ds(0, n)], target),
    ]
    copies = [pltpu.make_async_copy(a, b, sems.at[i]) for i, (a, b) in enumerate(pairs)]
    for c in copies:
        c.start()
    for c in copies[:2]:
        c.wait()
    predicted = times_transposed(right[...], left[...])
    for c in copies[2:]:
        c.wait()
    err = errors(predicted, target[...], codes[...], shifts[0:1, 0, 0:n], scale)
    error[...] = err
    out[...] = stepped(right[...], err, left[...], scale)


def second_kernel(n, scale, right_hbm, observed_hbm, left, codes, shifts,
                  out, error, right, following, target, sems):
    pairs = [
        (right_hbm.at[0, pl.ds(n, n)], right),
        (observed_hbm.at[0, 0, pl.ds(n, n)], target),
        (observed_hbm.at[0, 1, pl.ds(0, n)], following),
    ]
    copies = [pltpu.make_async_copy(a, b, sems.at[i]) for i, (a, b) in enumerate(pairs)]
    for c in copies:
        c.start()
    copies[0].wait()
    predicted = times_transposed(right[...], left[...])
    copies[1].wait()
    err = errors(predicted, target[...], codes[...], shifts[0:1, 0, n : 2 * n], scale)
    error[...] = err
    out[...] = stepped(right[...], err, left[...], scale)
    copies[2].wait()


def visit_kernel(s, a, n, scale, observed_hbm, right, left, target, codes, shifts, prior, out, error, following, sem):
    s_next, a_next = (s + 1, 0) if a else (s, n)
    copy = pltpu.make_async_copy(observed_hbm.at[0, s_next, pl.ds(a_next, n)], following, sem)
    copy.start()
    predicted = times_transposed(right[...], left[...])
    err = errors(predicted, target[...], codes[...], shifts[0:1, s, a : a + n], scale)
    error[...] = err
    out[...] = stepped(right[...], err, left[...], scale)
    copy.wait()


def last_kernel(s, a, n, scale, right, left, target, codes, shifts, prior, grad_sum, out, theirs, mine, total):
    half = left.shape[0] // 2
    core = lax.rem(lax.axis_index("lane"), 2)
    predicted = times_transposed(right[...], left[...])
    err = errors(predicted, target[...], codes[...], shifts[0:1, s, a : a + n], scale)
    total[...] = grad_sum[...] + lax.dot_general(
        err, right[...], (((0,), (0,)), ((), ())), preferred_element_type=f32
    )
    theirs[...] = total[pl.ds(pl.multiple_of((1 - core) * half, half), half), :].astype(bf16)
    mine[...] = total[pl.ds(pl.multiple_of(core * half, half), half), :]
    out[...] = stepped(right[...], err, left[...], scale)


def store_kernel(left, first, second, left_hbm, right_hbm, sems):
    n = first.shape[0]
    pairs = [(left, left_hbm), (first, right_hbm.at[0, pl.ds(0, n)]), (second, right_hbm.at[0, pl.ds(n, n)])]
    copies = [pltpu.make_async_copy(a, b, sems.at[i]) for i, (a, b) in enumerate(pairs)]
    for c in copies:
        c.start()
    for c in copies:
        c.wait()


def local(left_factor, right_factor, observed, row_codes, shift_codes):
    rows, w = left_factor.shape
    scale = 1.0 / math.sqrt(w)
    steps = observed.shape[1]
    n = right_factor.shape[1] // 2
    part, tile = pltpu.VMEM((n, w), bf16), pltpu.VMEM((n, rows), bf16)
    right_hbm, left_hbm, observed_hbm, codes_hbm, shifts_hbm = keep_hbm(
        right_factor, left_factor, observed, row_codes[None, :], shift_codes
    )
    after_a, error_a, right_a, plain_left, codes, shifts = pl.pallas_call(
        functools.partial(first_kernel, n, scale),
        out_shape=[part, tile, part, pltpu.VMEM((rows, w), bf16), pltpu.VMEM((1, rows), jnp.int32),
                   pltpu.VMEM(shift_codes.shape, jnp.int32)],
        in_specs=[in_hbm] * 5,
        out_specs=[in_vmem] * 6,
        scratch_shapes=[pltpu.VMEM((n, rows), bf16), pltpu.SemaphoreType.DMA((5,))],
        compiler_params=params,
        cost_estimate=cost(n, w, 2),
        name="first_visit",
    )(right_hbm, left_hbm, observed_hbm, codes_hbm, shifts_hbm)
    moving = [passed_along(after_a), None]
    left, codes, shifts = keep_vmem(plain_left, codes, shifts)
    after_b, error_b, right_b, following = pl.pallas_call(
        functools.partial(second_kernel, n, scale),
        out_shape=[part, tile, part, tile],
        in_specs=[in_hbm] * 2 + [in_vmem] * 3,
        out_specs=[in_vmem] * 4,
        scratch_shapes=[pltpu.VMEM((n, rows), bf16), pltpu.SemaphoreType.DMA((3,))],
        compiler_params=params,
        cost_estimate=cost(n, w, 2),
        name="second_visit",
    )(right_hbm, observed_hbm, left, codes, shifts)
    moving[1] = passed_along(after_b)

    def left_gradient(error, right):
        return lax.dot_general(error, right, (((0,), (0,)), ((), ())), preferred_element_type=f32)

    grad_sum = left_gradient(error_a, right_a) + left_gradient(error_b, right_b)
    parts, error = [None, None], error_b
    for s in range(1, steps):
        for i in range(2):
            right, = keep_vmem(moving[i])
            if s + 1 == steps and i == 1:
                grad_in, = keep_vmem(grad_sum)
                parts[i], theirs, mine = pl.pallas_call(
                    functools.partial(last_kernel, s, i * n, n, scale),
                    out_shape=[part, pltpu.VMEM((rows // 2, w), bf16), pltpu.VMEM((rows // 2, w), f32)],
                    in_specs=[in_vmem] * 7,
                    out_specs=[in_vmem] * 3,
                    scratch_shapes=[pltpu.VMEM((rows, w), f32)],
                    compiler_params=params,
                    cost_estimate=cost(n, w, 3),
                    name="last_visit",
                )(right, left, *keep_vmem(following), codes, shifts, *keep_vmem(error), grad_in)
                continue
            parts[i], error, following = pl.pallas_call(
                functools.partial(visit_kernel, s, i * n, n, scale),
                out_shape=[part, tile, tile],
                in_specs=[in_hbm] + [in_vmem] * 6,
                out_specs=[in_vmem] * 3,
                scratch_shapes=[pltpu.SemaphoreType.DMA],
                compiler_params=params,
                cost_estimate=cost(n, w, 2),
                name="visit",
            )(observed_hbm, right, left, *keep_vmem(following), codes, shifts, *keep_vmem(error))
            grad_sum = grad_sum + left_gradient(error, moving[i])
            if s + 1 < steps:
                moving[i] = passed_along(parts[i])

    half = rows // 2
    core = lax.axis_index("lane") % 2
    own_rows = lax.dynamic_slice_in_dim(plain_left, core * half, half, 0)
    sent = both(theirs, 1)
    chip_sum = mine + jnp.where(core == 0, sent[1], sent[0]).astype(f32)
    sums = both(chip_sum.astype(bf16), 2).astype(f32)
    renewed = own_rows.astype(f32) - step_left * scale * (sums[0] + sums[1])
    new_left = both(renewed.astype(bf16), 1).reshape(rows, w)
    return tuple(
        pl.pallas_call(
            store_kernel,
            out_shape=[jax.ShapeDtypeStruct((rows, w), bf16), jax.ShapeDtypeStruct(right_factor.shape, bf16)],
            in_specs=[in_vmem] * 3,
            out_specs=[in_hbm] * 2,
            scratch_shapes=[pltpu.SemaphoreType.DMA((3,))],
            compiler_params=params,
            name="store",
        )(*keep_vmem(new_left, *parts))
    )


def solution(mesh):
    in_specs = (
        P("blk", None),
        P("lane", "blk", None),
        P("lane", None, None, "blk"),
        P("blk"),
        P("lane", None, "blk"),
    )
    out_specs = (P("blk", None), P("lane", "blk", None))
    return jax.shard_map(local, mesh=mesh, in_specs=in_specs, out_specs=out_specs, check_vma=False)
```

```python
import functools
import math

import jax
import jax.numpy as jnp
from jax import lax
from jax.experimental import pallas as pl
from jax.experimental.pallas import tpu as pltpu
from jax.sharding import PartitionSpec as P

step_right = 0.25
step_left = 0.1
f32 = jnp.float32
bf16 = jnp.bfloat16
vmem_bytes = 12 << 20
chunk_rows = (256, 256)
in_vmem = pl.BlockSpec(memory_space=pltpu.VMEM)
in_hbm = pl.BlockSpec(memory_space=pltpu.HBM)
costs = (1, 1, 1, 1)


def price(s):
    return pl.CostEstimate(flops=int(costs[s] * 2e8), bytes_accessed=int(costs[s] * 1e6), transcendentals=0)


params = pltpu.CompilerParams(vmem_limit_bytes=vmem_bytes)


def passed_along(value):
    count = lax.axis_size("blk")
    return lax.ppermute(value, "blk", [(i, (i + 1) % count) for i in range(count)])


def both(value, bit):
    groups = [[i, i ^ bit] for i in range(lax.axis_size("lane")) if i < i ^ bit]
    return lax.all_gather(value, "lane", axis=0, axis_index_groups=groups, tiled=False)


def keep_hbm(*arrays):
    return [pltpu.with_memory_space_constraint(x, pltpu.HBM) for x in arrays]


def keep_vmem(*arrays):
    return [pltpu.with_memory_space_constraint(x, pltpu.VMEM) for x in arrays]


def times_transposed(a, left):
    return lax.dot_general(a, left, (((1,), (1,)), ((), ())), preferred_element_type=f32)


def errors(predicted, target, codes, shifts, scale):
    rows, columns = predicted.shape
    by_row = jnp.broadcast_to(shifts, (128, rows)).T
    by_row = jnp.concatenate([by_row] * (columns // 128), axis=1)
    bits = jnp.right_shift(jnp.broadcast_to(codes, (rows, columns)), by_row) & 1
    return jnp.where(bits == 1, predicted * scale - target.astype(f32), 0.0).astype(bf16)


def stepped(right, error, left, scale):
    grad = jnp.dot(error, left, preferred_element_type=f32)
    return (right.astype(f32) - step_right * scale * grad).astype(bf16)


def first_kernel(spans, scale, right_hbm, left_hbm, observed_hbm, codes_hbm, shifts_hbm, out, error, left, codes, shifts, *refs):
    count = len(spans)
    rights, others, target, sems = refs[:count], refs[count : 2 * count - 1], refs[-2], refs[-1]
    pairs = [
        (right_hbm.at[0, pl.ds(*spans[0])], rights[0]),
        (left_hbm, left),
        (observed_hbm.at[0, 0, pl.ds(*spans[0])], target),
        (codes_hbm, codes),
        (shifts_hbm, shifts),
    ]
    for i in range(1, count):
        pairs.append((right_hbm.at[0, pl.ds(*spans[i])], rights[i]))
        pairs.append((observed_hbm.at[0, 0, pl.ds(*spans[i])], others[i - 1]))
    copies = [pltpu.make_async_copy(a, b, sems.at[i]) for i, (a, b) in enumerate(pairs)]
    for c in copies:
        c.start()
    for c in copies[:2]:
        c.wait()
    right = rights[0][...]
    predicted = times_transposed(right, left[...])
    for c in copies[2:5]:
        c.wait()
    err = errors(predicted, target[...], codes[...], shifts[0:1, 0, 0 : spans[0][1]], scale)
    error[...] = err
    out[...] = stepped(right, err, left[...], scale)
    for c in copies[5:]:
        c.wait()


def visit_kernel(s, a, n, scale, right, left, target, codes, shifts, prior, out, error):
    predicted = times_transposed(right[...], left[...])
    err = errors(predicted, target[...], codes[...], shifts[0:1, s, a : a + n], scale)
    error[...] = err
    out[...] = stepped(right[...], err, left[...], scale)


def gradient_kernel(s, spans, observed_hbm, *refs):
    count = len(spans)
    errors_rights, rest = refs[: 2 * count], refs[2 * count :]
    before, out, following, sems = rest[: -count - 2], rest[-count - 2], rest[-count - 1 : -1], rest[-1]
    copies = [
        pltpu.make_async_copy(observed_hbm.at[0, s + 1, pl.ds(*spans[i])], ref, sems.at[i])
        for i, ref in enumerate(following)
    ]
    for c in copies:
        c.start()
    total = before[0][...] if before else None
    for i in range(count):
        error, right = errors_rights[2 * i : 2 * i + 2]
        term = lax.dot_general(error[...], right[...], (((0,), (0,)), ((), ())), preferred_element_type=f32)
        total = term if total is None else total + term
    out[...] = total
    for c in copies:
        c.wait()


def last_kernel(s, a, n, scale, right, left, target, codes, shifts, prior, grad_sum, out, theirs, mine, error):
    half = left.shape[0] // 2
    core = lax.rem(lax.axis_index("lane"), 2)
    predicted = times_transposed(right[...], left[...])
    err = errors(predicted, target[...], codes[...], shifts[0:1, s, a : a + n], scale)
    error[...] = err
    for ref, which in ((theirs, 1 - core), (mine, core)):
        own = pl.ds(pl.multiple_of(which * half, half), half)
        term = lax.dot_general(
            error[:, own], right[...], (((0,), (0,)), ((), ())), preferred_element_type=f32
        )
        ref[...] = (grad_sum[own, :] + term).astype(ref.dtype)
    out[...] = stepped(right[...], err, left[...], scale)


def settle_kernel(s, a, n, scale, right, left, target, codes, shifts, prior, right_out, error, fresh, sem):
    visit_kernel(s, a, n, scale, right, left, target, codes, shifts, prior, fresh, error)
    copy = pltpu.make_async_copy(fresh, right_out.at[0, pl.ds(a, n)], sem)
    copy.start()
    copy.wait()


def combine_kernel(mine, sent, out):
    core = lax.rem(lax.axis_index("lane"), 2)
    out[...] = (mine[...] + sent[1 - core].astype(f32)).astype(bf16)


def renew_kernel(scale, sums, left, out):
    half = out.shape[0]
    core = lax.rem(lax.axis_index("lane"), 2)
    own = left[pl.ds(pl.multiple_of(core * half, half), half), :].astype(f32)
    total = sums[0].astype(f32) + sums[1].astype(f32)
    out[...] = (own - step_left * scale * total).astype(bf16)


def store_kernel(first, left, part, right_hbm, left_hbm, right_out, sems):
    pairs = [(left, left_hbm), (part, right_out.at[0, pl.ds(first, part.shape[0])])]
    copies = [pltpu.make_async_copy(a, b, sems.at[i]) for i, (a, b) in enumerate(pairs)]
    for c in copies:
        c.start()
    for c in copies:
        c.wait()


def local(left_factor, right_factor, observed, row_codes, shift_codes):
    rows, w = left_factor.shape
    scale = 1.0 / math.sqrt(w)
    steps = observed.shape[1]
    spans = [(sum(chunk_rows[:i]), n) for i, n in enumerate(chunk_rows)]
    count = len(spans)
    parts_of = [pltpu.VMEM((n, w), bf16) for _, n in spans]
    tiles = [pltpu.VMEM((n, rows), bf16) for _, n in spans]
    right_hbm, left_hbm, observed_hbm, codes_hbm, shifts_hbm = keep_hbm(
        right_factor, left_factor, observed, row_codes[None, :], shift_codes
    )
    after, error, plain_left, codes, shifts, *loaded = pl.pallas_call(
        functools.partial(first_kernel, spans, scale),
        out_shape=[parts_of[0], tiles[0], pltpu.VMEM((rows, w), bf16), pltpu.VMEM((1, rows), jnp.int32),
                   pltpu.VMEM(shift_codes.shape, jnp.int32), *parts_of, *tiles[1:]],
        in_specs=[in_hbm] * 5,
        out_specs=[in_vmem] * (2 * count + 4),
        scratch_shapes=[tiles[0], pltpu.SemaphoreType.DMA((2 * count + 3,))],
        compiler_params=params,
        cost_estimate=price(0),
        name="first_visit",
    )(right_hbm, left_hbm, observed_hbm, codes_hbm, shifts_hbm)
    left, codes, shifts = keep_vmem(plain_left, codes, shifts)

    def visit(s, i, right, target, prior):
        right, target, prior = keep_vmem(right, target, prior)
        return pl.pallas_call(
            functools.partial(visit_kernel, s, *spans[i], scale),
            out_shape=[parts_of[i], tiles[i]],
            in_specs=[in_vmem] * 6,
            out_specs=[in_vmem] * 2,
            input_output_aliases={2: 1},
            compiler_params=params,
            cost_estimate=price(s),
            name="visit",
        )(right, left, target, codes, shifts, prior)

    moving, held = [passed_along(after)], [error, loaded[0]]
    for i in range(1, count):
        after, error = visit(0, i, loaded[i], loaded[count + i - 1], error)
        moving.append(passed_along(after))
        held += [error, loaded[i]]

    def gradient(s, *operands):
        added = len(operands) > 2 * count
        return pl.pallas_call(
            functools.partial(gradient_kernel, s, spans),
            out_shape=[pltpu.VMEM((rows, w), f32), *tiles],
            in_specs=[in_hbm] + [in_vmem] * len(operands),
            out_specs=[in_vmem] * (count + 1),
            scratch_shapes=[pltpu.SemaphoreType.DMA((count,))],
            input_output_aliases={2 * count + 1: 0} if added else {},
            compiler_params=params,
            cost_estimate=price(s),
            name="gradient",
        )(observed_hbm, *keep_vmem(*operands))

    grad_sum, *following = gradient(0, *held)
    parts = [None] * count
    for s in range(1, steps):
        held = []
        for i in range(count):
            right, = keep_vmem(moving[i])
            if s + 1 == steps and i + 1 == count:
                grad_in, = keep_vmem(grad_sum)
                parts[i], theirs, mine = pl.pallas_call(
                    functools.partial(last_kernel, s, *spans[i], scale),
                    out_shape=[parts_of[i], pltpu.VMEM((rows // 2, w), bf16), pltpu.VMEM((rows // 2, w), f32)],
                    in_specs=[in_vmem] * 7,
                    out_specs=[in_vmem] * 3,
                    scratch_shapes=[tiles[i]],
                    compiler_params=params,
                    cost_estimate=price(s),
                    name="last_visit",
                )(right, left, *keep_vmem(following[i]), codes, shifts, *keep_vmem(error), grad_in)
                continue
            if s + 1 < steps:
                parts[i], error = visit(s, i, moving[i], following[i], error)
            else:
                right_out, error = pl.pallas_call(
                    functools.partial(settle_kernel, s, *spans[i], scale),
                    out_shape=[pltpu.HBM(right_factor.shape, bf16), tiles[i]],
                    in_specs=[in_vmem] * 6,
                    out_specs=[in_hbm, in_vmem],
                    scratch_shapes=[parts_of[i], pltpu.SemaphoreType.DMA],
                    input_output_aliases={2: 1},
                    compiler_params=params,
                    cost_estimate=price(s),
                    name="settle",
                )(right, left, *keep_vmem(following[i]), codes, shifts, *keep_vmem(error))
            held += [error, moving[i]]
            if s + 1 < steps:
                moving[i] = passed_along(parts[i])
            else:
                grad_sum = grad_sum + lax.dot_general(
                    error, held[-1], (((0,), (0,)), ((), ())), preferred_element_type=f32
                )
        if s + 1 < steps:
            grad_sum, *following = gradient(s, *held, grad_sum)

    half = pltpu.VMEM((rows // 2, w), bf16)
    chip_sum = pl.pallas_call(
        combine_kernel, out_shape=half, in_specs=[in_vmem] * 2, out_specs=in_vmem, compiler_params=params, name="combine"
    )(*keep_vmem(mine, both(theirs, 1)))
    renewed = pl.pallas_call(
        functools.partial(renew_kernel, scale), out_shape=half, in_specs=[in_vmem] * 2, out_specs=in_vmem,
        compiler_params=params, name="renew"
    )(*keep_vmem(both(chip_sum, 2)), left)
    new_left = both(renewed, 1).reshape(rows, w)
    return tuple(
        pl.pallas_call(
            functools.partial(store_kernel, spans[-1][0]),
            out_shape=[jax.ShapeDtypeStruct((rows, w), bf16), jax.ShapeDtypeStruct(right_factor.shape, bf16)],
            in_specs=[in_vmem] * 2 + [in_hbm],
            out_specs=[in_hbm] * 2,
            scratch_shapes=[pltpu.SemaphoreType.DMA((2,))],
            input_output_aliases={2: 1},
            compiler_params=params,
            name="store",
        )(*keep_vmem(new_left, parts[-1]), *keep_hbm(right_out))
    )


def solution(mesh):
    in_specs = (
        P("blk", None),
        P("lane", "blk", None),
        P("lane", None, None, "blk"),
        P("blk"),
        P("lane", None, "blk"),
    )
    out_specs = (P("blk", None), P("lane", "blk", None))
    return jax.shard_map(local, mesh=mesh, in_specs=in_specs, out_specs=out_specs, check_vma=False)
```

```python
import functools
import math

import jax
import jax.numpy as jnp
from jax import lax
from jax.experimental import pallas as pl
from jax.experimental.pallas import tpu as pltpu
from jax.sharding import PartitionSpec as P

step_right = 0.25
step_left = 0.1
f32 = jnp.float32
bf16 = jnp.bfloat16
vmem_bytes = 12 << 20
chunk_rows = (256, 256)
in_vmem = pl.BlockSpec(memory_space=pltpu.VMEM)
in_hbm = pl.BlockSpec(memory_space=pltpu.HBM)
costs = (1, 1, 1, 1)


def price(s):
    return pl.CostEstimate(flops=int(costs[s] * 2e8), bytes_accessed=int(costs[s] * 1e6), transcendentals=0)


params = pltpu.CompilerParams(vmem_limit_bytes=vmem_bytes)


def passed_along(value):
    count = lax.axis_size("blk")
    return lax.ppermute(value, "blk", [(i, (i + 1) % count) for i in range(count)])


def both(value, bit):
    groups = [[i, i ^ bit] for i in range(lax.axis_size("lane")) if i < i ^ bit]
    return lax.all_gather(value, "lane", axis=0, axis_index_groups=groups, tiled=False)


def keep_hbm(*arrays):
    return [pltpu.with_memory_space_constraint(x, pltpu.HBM) for x in arrays]


def keep_vmem(*arrays):
    return [pltpu.with_memory_space_constraint(x, pltpu.VMEM) for x in arrays]


def times_transposed(a, left):
    return lax.dot_general(a, left, (((1,), (1,)), ((), ())), preferred_element_type=f32)


def errors(predicted, target, codes, shifts, scale):
    rows, columns = predicted.shape
    by_row = jnp.broadcast_to(shifts, (128, rows)).T
    by_row = jnp.concatenate([by_row] * (columns // 128), axis=1)
    bits = jnp.right_shift(jnp.broadcast_to(codes, (rows, columns)), by_row) & 1
    return jnp.where(bits == 1, predicted * scale - target.astype(f32), 0.0).astype(bf16)


def stepped(right, error, left, scale):
    grad = jnp.dot(error, left, preferred_element_type=f32)
    return (right.astype(f32) - step_right * scale * grad).astype(bf16)


def first_kernel(spans, scale, right_hbm, left_hbm, observed_hbm, codes_hbm, shifts_hbm, out, error, left, codes, shifts, *refs):
    count = len(spans)
    rights, others, target, sems = refs[:count], refs[count : 2 * count - 1], refs[-2], refs[-1]
    pairs = [
        (right_hbm.at[0, pl.ds(*spans[0])], rights[0]),
        (left_hbm, left),
        (observed_hbm.at[0, 0, pl.ds(*spans[0])], target),
        (codes_hbm, codes),
        (shifts_hbm, shifts),
    ]
    for i in range(1, count):
        pairs.append((right_hbm.at[0, pl.ds(*spans[i])], rights[i]))
        pairs.append((observed_hbm.at[0, 0, pl.ds(*spans[i])], others[i - 1]))
    copies = [pltpu.make_async_copy(a, b, sems.at[i]) for i, (a, b) in enumerate(pairs)]
    for c in copies:
        c.start()
    for c in copies[:2]:
        c.wait()
    right = rights[0][...]
    predicted = times_transposed(right, left[...])
    for c in copies[2:5]:
        c.wait()
    err = errors(predicted, target[...], codes[...], shifts[0:1, 0, 0 : spans[0][1]], scale)
    error[...] = err
    out[...] = stepped(right, err, left[...], scale)
    for c in copies[5:]:
        c.wait()


def visit_kernel(s, a, n, scale, right, left, turned, target, codes, shifts, prior, out, error):
    predicted = times_transposed(right[...], left[...]) if s == 0 else jnp.dot(
        right[...], turned[...], preferred_element_type=f32
    )
    err = errors(predicted, target[...], codes[...], shifts[0:1, s, a : a + n], scale)
    error[...] = err
    out[...] = stepped(right[...], err, left[...], scale)


def gradient_kernel(s, spans, observed_hbm, *refs):
    count = len(spans)
    errors_rights, rest = refs[: 2 * count], refs[2 * count :]
    before, out, following, sems = rest[: -count - 2], rest[-count - 2], rest[-count - 1 : -1], rest[-1]
    copies = [
        pltpu.make_async_copy(observed_hbm.at[0, s + 1, pl.ds(*spans[i])], ref, sems.at[i])
        for i, ref in enumerate(following)
    ]
    for c in copies:
        c.start()
    total = before[0][...] if before else None
    for i in range(count):
        error, right = errors_rights[2 * i : 2 * i + 2]
        term = lax.dot_general(error[...], right[...], (((0,), (0,)), ((), ())), preferred_element_type=f32)
        total = term if total is None else total + term
    out[...] = total
    for c in copies:
        c.wait()


def turn_kernel(left, prior, out):
    out[...] = left[...].T


def last_kernel(s, a, n, scale, right, left, turned, target, codes, shifts, prior, grad_sum, out, theirs, mine, error):
    half = left.shape[0] // 2
    core = lax.rem(lax.axis_index("lane"), 2)
    predicted = jnp.dot(right[...], turned[...], preferred_element_type=f32)
    err = errors(predicted, target[...], codes[...], shifts[0:1, s, a : a + n], scale)
    error[...] = err
    for ref, which in ((theirs, 1 - core), (mine, core)):
        own = pl.ds(pl.multiple_of(which * half, half), half)
        term = lax.dot_general(
            error[:, own], right[...], (((0,), (0,)), ((), ())), preferred_element_type=f32
        )
        ref[...] = (grad_sum[own, :] + term).astype(ref.dtype)
    out[...] = stepped(right[...], err, left[...], scale)


def settle_kernel(s, a, n, scale, right, left, turned, target, codes, shifts, prior, right_out, error, fresh, sem):
    visit_kernel(s, a, n, scale, right, left, turned, target, codes, shifts, prior, fresh, error)
    copy = pltpu.make_async_copy(fresh, right_out.at[0, pl.ds(a, n)], sem)
    copy.start()
    copy.wait()


def combine_kernel(mine, sent, out):
    core = lax.rem(lax.axis_index("lane"), 2)
    out[...] = (mine[...] + sent[1 - core].astype(f32)).astype(bf16)


def renew_kernel(scale, sums, left, out):
    half = out.shape[0]
    core = lax.rem(lax.axis_index("lane"), 2)
    own = left[pl.ds(pl.multiple_of(core * half, half), half), :].astype(f32)
    total = sums[0].astype(f32) + sums[1].astype(f32)
    out[...] = (own - step_left * scale * total).astype(bf16)


def store_kernel(first, left, part, right_hbm, left_hbm, right_out, sems):
    pairs = [(left, left_hbm), (part, right_out.at[0, pl.ds(first, part.shape[0])])]
    copies = [pltpu.make_async_copy(a, b, sems.at[i]) for i, (a, b) in enumerate(pairs)]
    for c in copies:
        c.start()
    for c in copies:
        c.wait()


def local(left_factor, right_factor, observed, row_codes, shift_codes):
    rows, w = left_factor.shape
    scale = 1.0 / math.sqrt(w)
    steps = observed.shape[1]
    spans = [(sum(chunk_rows[:i]), n) for i, n in enumerate(chunk_rows)]
    count = len(spans)
    parts_of = [pltpu.VMEM((n, w), bf16) for _, n in spans]
    tiles = [pltpu.VMEM((n, rows), bf16) for _, n in spans]
    right_hbm, left_hbm, observed_hbm, codes_hbm, shifts_hbm = keep_hbm(
        right_factor, left_factor, observed, row_codes[None, :], shift_codes
    )
    after, error, plain_left, codes, shifts, *loaded = pl.pallas_call(
        functools.partial(first_kernel, spans, scale),
        out_shape=[parts_of[0], tiles[0], pltpu.VMEM((rows, w), bf16), pltpu.VMEM((1, rows), jnp.int32),
                   pltpu.VMEM(shift_codes.shape, jnp.int32), *parts_of, *tiles[1:]],
        in_specs=[in_hbm] * 5,
        out_specs=[in_vmem] * (2 * count + 4),
        scratch_shapes=[tiles[0], pltpu.SemaphoreType.DMA((2 * count + 3,))],
        compiler_params=params,
        cost_estimate=price(0),
        name="first_visit",
    )(right_hbm, left_hbm, observed_hbm, codes_hbm, shifts_hbm)
    left, codes, shifts = keep_vmem(plain_left, codes, shifts)

    def visit(s, i, right, target, prior):
        right, target, prior = keep_vmem(right, target, prior)
        return pl.pallas_call(
            functools.partial(visit_kernel, s, *spans[i], scale),
            out_shape=[parts_of[i], tiles[i]],
            in_specs=[in_vmem] * 7,
            out_specs=[in_vmem] * 2,
            input_output_aliases={3: 1},
            compiler_params=params,
            cost_estimate=price(s),
            name="visit",
        )(right, left, turned[0], target, codes, shifts, prior)

    turned = [left]
    moving, held = [passed_along(after)], [error, loaded[0]]
    for i in range(1, count):
        after, error = visit(0, i, loaded[i], loaded[count + i - 1], error)
        moving.append(passed_along(after))
        held += [error, loaded[i]]

    def gradient(s, *operands):
        added = len(operands) > 2 * count
        return pl.pallas_call(
            functools.partial(gradient_kernel, s, spans),
            out_shape=[pltpu.VMEM((rows, w), f32), *tiles],
            in_specs=[in_hbm] + [in_vmem] * len(operands),
            out_specs=[in_vmem] * (count + 1),
            scratch_shapes=[pltpu.SemaphoreType.DMA((count,))],
            input_output_aliases={2 * count + 1: 0} if added else {},
            compiler_params=params,
            cost_estimate=price(s),
            name="gradient",
        )(observed_hbm, *keep_vmem(*operands))

    turned = keep_vmem(
        pl.pallas_call(
            turn_kernel, out_shape=pltpu.VMEM((w, rows), bf16), in_specs=[in_vmem] * 2, out_specs=in_vmem,
            compiler_params=params, cost_estimate=price(0), name="turn"
        )(left, *keep_vmem(error))
    )
    grad_sum, *following = gradient(0, *held)
    parts = [None] * count
    for s in range(1, steps):
        held = []
        for i in range(count):
            right, = keep_vmem(moving[i])
            if s + 1 == steps and i + 1 == count:
                grad_in, = keep_vmem(grad_sum)
                parts[i], theirs, mine = pl.pallas_call(
                    functools.partial(last_kernel, s, *spans[i], scale),
                    out_shape=[parts_of[i], pltpu.VMEM((rows // 2, w), bf16), pltpu.VMEM((rows // 2, w), f32)],
                    in_specs=[in_vmem] * 8,
                    out_specs=[in_vmem] * 3,
                    scratch_shapes=[tiles[i]],
                    compiler_params=params,
                    cost_estimate=price(s),
                    name="last_visit",
                )(right, left, turned[0], *keep_vmem(following[i]), codes, shifts, *keep_vmem(error), grad_in)
                continue
            if s + 1 < steps:
                parts[i], error = visit(s, i, moving[i], following[i], error)
            else:
                right_out, error = pl.pallas_call(
                    functools.partial(settle_kernel, s, *spans[i], scale),
                    out_shape=[pltpu.HBM(right_factor.shape, bf16), tiles[i]],
                    in_specs=[in_vmem] * 7,
                    out_specs=[in_hbm, in_vmem],
                    scratch_shapes=[parts_of[i], pltpu.SemaphoreType.DMA],
                    input_output_aliases={3: 1},
                    compiler_params=params,
                    cost_estimate=price(s),
                    name="settle",
                )(right, left, turned[0], *keep_vmem(following[i]), codes, shifts, *keep_vmem(error))
            held += [error, moving[i]]
            if s + 1 < steps:
                moving[i] = passed_along(parts[i])
            else:
                grad_sum = grad_sum + lax.dot_general(
                    error, held[-1], (((0,), (0,)), ((), ())), preferred_element_type=f32
                )
        if s + 1 < steps:
            grad_sum, *following = gradient(s, *held, grad_sum)

    half = pltpu.VMEM((rows // 2, w), bf16)
    chip_sum = pl.pallas_call(
        combine_kernel, out_shape=half, in_specs=[in_vmem] * 2, out_specs=in_vmem, compiler_params=params, name="combine"
    )(*keep_vmem(mine, both(theirs, 1)))
    renewed = pl.pallas_call(
        functools.partial(renew_kernel, scale), out_shape=half, in_specs=[in_vmem] * 2, out_specs=in_vmem,
        compiler_params=params, name="renew"
    )(*keep_vmem(both(chip_sum, 2)), left)
    new_left = both(renewed, 1).reshape(rows, w)
    return tuple(
        pl.pallas_call(
            functools.partial(store_kernel, spans[-1][0]),
            out_shape=[jax.ShapeDtypeStruct((rows, w), bf16), jax.ShapeDtypeStruct(right_factor.shape, bf16)],
            in_specs=[in_vmem] * 2 + [in_hbm],
            out_specs=[in_hbm] * 2,
            scratch_shapes=[pltpu.SemaphoreType.DMA((2,))],
            input_output_aliases={2: 1},
            compiler_params=params,
            name="store",
        )(*keep_vmem(new_left, parts[-1]), *keep_hbm(right_out))
    )


def solution(mesh):
    in_specs = (
        P("blk", None),
        P("lane", "blk", None),
        P("lane", None, None, "blk"),
        P("blk"),
        P("lane", None, "blk"),
    )
    out_specs = (P("blk", None), P("lane", "blk", None))
    return jax.shard_map(local, mesh=mesh, in_specs=in_specs, out_specs=out_specs, check_vma=False)
```

```python
import functools
import math

import jax
import jax.numpy as jnp
from jax import lax
from jax.experimental import pallas as pl
from jax.experimental.pallas import tpu as pltpu
from jax.sharding import PartitionSpec as P

step_right = 0.25
step_left = 0.1
f32 = jnp.float32
bf16 = jnp.bfloat16
vmem_bytes = 12 << 20
chunk_rows = (256, 256)
in_vmem = pl.BlockSpec(memory_space=pltpu.VMEM)
in_hbm = pl.BlockSpec(memory_space=pltpu.HBM)
costs = (1, 1, 1, 1)


def price(s):
    return pl.CostEstimate(flops=int(costs[s] * 2e8), bytes_accessed=int(costs[s] * 1e6), transcendentals=0)


params = pltpu.CompilerParams(vmem_limit_bytes=vmem_bytes)


def passed_along(value):
    count = lax.axis_size("blk")
    return lax.ppermute(value, "blk", [(i, (i + 1) % count) for i in range(count)])


def both(value, bit):
    groups = [[i, i ^ bit] for i in range(lax.axis_size("lane")) if i < i ^ bit]
    return lax.all_gather(value, "lane", axis=0, axis_index_groups=groups, tiled=False)


def keep_hbm(*arrays):
    return [pltpu.with_memory_space_constraint(x, pltpu.HBM) for x in arrays]


def keep_vmem(*arrays):
    return [pltpu.with_memory_space_constraint(x, pltpu.VMEM) for x in arrays]


def times_transposed(a, left):
    return lax.dot_general(a, left, (((1,), (1,)), ((), ())), preferred_element_type=f32)


def errors(predicted, target, codes, shifts, scale):
    rows, columns = predicted.shape
    by_row = jnp.broadcast_to(shifts, (128, rows)).T
    by_row = jnp.concatenate([by_row] * (columns // 128), axis=1)
    bits = jnp.right_shift(jnp.broadcast_to(codes, (rows, columns)), by_row) & 1
    return jnp.where(bits == 1, predicted * scale - target.astype(f32), 0.0).astype(bf16)


def stepped(right, error, left, scale):
    grad = jnp.dot(error, left, preferred_element_type=f32)
    return (right.astype(f32) - step_right * scale * grad).astype(bf16)


def first_kernel(spans, scale, right_hbm, left_hbm, observed_hbm, codes_hbm, shifts_hbm, out, error, left, codes, shifts, *refs):
    count = len(spans)
    rights, others, target, sems = refs[:count], refs[count : 2 * count - 1], refs[-2], refs[-1]
    pairs = [
        (right_hbm.at[0, pl.ds(*spans[0])], rights[0]),
        (left_hbm, left),
        (observed_hbm.at[0, 0, pl.ds(*spans[0])], target),
        (codes_hbm, codes),
        (shifts_hbm, shifts),
    ]
    for i in range(1, count):
        pairs.append((right_hbm.at[0, pl.ds(*spans[i])], rights[i]))
        pairs.append((observed_hbm.at[0, 0, pl.ds(*spans[i])], others[i - 1]))
    copies = [pltpu.make_async_copy(a, b, sems.at[i]) for i, (a, b) in enumerate(pairs)]
    for c in copies:
        c.start()
    for c in copies[:2]:
        c.wait()
    right = rights[0][...]
    predicted = times_transposed(right, left[...])
    for c in copies[2:5]:
        c.wait()
    err = errors(predicted, target[...], codes[...], shifts[0:1, 0, 0 : spans[0][1]], scale)
    error[...] = err
    out[...] = stepped(right, err, left[...], scale)
    for c in copies[5:]:
        c.wait()


def visit_kernel(s, a, n, scale, right, left, turned, target, codes, shifts, prior, out, error):
    predicted = times_transposed(right[...], left[...]) if s == 0 else jnp.dot(
        right[...], turned[...], preferred_element_type=f32
    )
    err = errors(predicted, target[...], codes[...], shifts[0:1, s, a : a + n], scale)
    error[...] = err
    out[...] = stepped(right[...], err, left[...], scale)


def gradient_kernel(s, spans, observed_hbm, *refs):
    count = len(spans)
    errors_rights, rest = refs[: 2 * count], refs[2 * count :]
    before, out, following, sems = rest[: -count - 2], rest[-count - 2], rest[-count - 1 : -1], rest[-1]
    copies = [
        pltpu.make_async_copy(observed_hbm.at[0, s + 1, pl.ds(*spans[i])], ref, sems.at[i])
        for i, ref in enumerate(following)
    ]
    for c in copies:
        c.start()
    total = before[0][...] if before else None
    for i in range(count):
        error, right = errors_rights[2 * i : 2 * i + 2]
        term = lax.dot_general(error[...], right[...], (((0,), (0,)), ((), ())), preferred_element_type=f32)
        total = term if total is None else total + term
    out[...] = total
    for c in copies:
        c.wait()


def turn_kernel(left, prior, out):
    out[...] = left[...].T


def last_kernel(s, a, n, scale, right, left, turned, target, codes, shifts, prior, grad_sum, error, theirs, mine):
    half = left.shape[0] // 2
    core = lax.rem(lax.axis_index("lane"), 2)
    predicted = jnp.dot(right[...], turned[...], preferred_element_type=f32)
    err = errors(predicted, target[...], codes[...], shifts[0:1, s, a : a + n], scale)
    error[...] = err
    for ref, which in ((theirs, 1 - core), (mine, core)):
        own = pl.ds(pl.multiple_of(which * half, half), half)
        term = lax.dot_general(
            error[:, own], right[...], (((0,), (0,)), ((), ())), preferred_element_type=f32
        )
        ref[...] = (grad_sum[own, :] + term).astype(ref.dtype)


def settle_kernel(s, a, n, scale, right, left, turned, target, codes, shifts, prior, right_out, error, fresh, sem):
    visit_kernel(s, a, n, scale, right, left, turned, target, codes, shifts, prior, fresh, error)
    copy = pltpu.make_async_copy(fresh, right_out.at[0, pl.ds(a, n)], sem)
    copy.start()
    copy.wait()


def combine_kernel(mine, sent, out):
    core = lax.rem(lax.axis_index("lane"), 2)
    out[...] = (mine[...] + sent[1 - core].astype(f32)).astype(bf16)


def renew_kernel(scale, sums, left, out):
    half = out.shape[0]
    core = lax.rem(lax.axis_index("lane"), 2)
    own = left[pl.ds(pl.multiple_of(core * half, half), half), :].astype(f32)
    total = sums[0].astype(f32) + sums[1].astype(f32)
    out[...] = (own - step_left * scale * total).astype(bf16)


def store_kernel(first, scale, new_left, right, error, left, right_hbm, left_hbm, right_out, fresh, sems):
    copies = [
        pltpu.make_async_copy(new_left, left_hbm, sems.at[0]),
        pltpu.make_async_copy(fresh, right_out.at[0, pl.ds(first, fresh.shape[0])], sems.at[1]),
    ]
    copies[0].start()
    fresh[...] = stepped(right[...], error[...], left[...], scale)
    copies[1].start()
    for c in copies:
        c.wait()


def local(left_factor, right_factor, observed, row_codes, shift_codes):
    rows, w = left_factor.shape
    scale = 1.0 / math.sqrt(w)
    steps = observed.shape[1]
    spans = [(sum(chunk_rows[:i]), n) for i, n in enumerate(chunk_rows)]
    count = len(spans)
    parts_of = [pltpu.VMEM((n, w), bf16) for _, n in spans]
    tiles = [pltpu.VMEM((n, rows), bf16) for _, n in spans]
    right_hbm, left_hbm, observed_hbm, codes_hbm, shifts_hbm = keep_hbm(
        right_factor, left_factor, observed, row_codes[None, :], shift_codes
    )
    after, error, plain_left, codes, shifts, *loaded = pl.pallas_call(
        functools.partial(first_kernel, spans, scale),
        out_shape=[parts_of[0], tiles[0], pltpu.VMEM((rows, w), bf16), pltpu.VMEM((1, rows), jnp.int32),
                   pltpu.VMEM(shift_codes.shape, jnp.int32), *parts_of, *tiles[1:]],
        in_specs=[in_hbm] * 5,
        out_specs=[in_vmem] * (2 * count + 4),
        scratch_shapes=[tiles[0], pltpu.SemaphoreType.DMA((2 * count + 3,))],
        compiler_params=params,
        cost_estimate=price(0),
        name="first_visit",
    )(right_hbm, left_hbm, observed_hbm, codes_hbm, shifts_hbm)
    left, codes, shifts = keep_vmem(plain_left, codes, shifts)

    def visit(s, i, right, target, prior):
        right, target, prior = keep_vmem(right, target, prior)
        return pl.pallas_call(
            functools.partial(visit_kernel, s, *spans[i], scale),
            out_shape=[parts_of[i], tiles[i]],
            in_specs=[in_vmem] * 7,
            out_specs=[in_vmem] * 2,
            input_output_aliases={3: 1},
            compiler_params=params,
            cost_estimate=price(s),
            name="visit",
        )(right, left, turned[0], target, codes, shifts, prior)

    turned = [left]
    moving, held = [passed_along(after)], [error, loaded[0]]
    for i in range(1, count):
        after, error = visit(0, i, loaded[i], loaded[count + i - 1], error)
        moving.append(passed_along(after))
        held += [error, loaded[i]]

    def gradient(s, *operands):
        added = len(operands) > 2 * count
        return pl.pallas_call(
            functools.partial(gradient_kernel, s, spans),
            out_shape=[pltpu.VMEM((rows, w), f32), *tiles],
            in_specs=[in_hbm] + [in_vmem] * len(operands),
            out_specs=[in_vmem] * (count + 1),
            scratch_shapes=[pltpu.SemaphoreType.DMA((count,))],
            input_output_aliases={2 * count + 1: 0} if added else {},
            compiler_params=params,
            cost_estimate=price(s),
            name="gradient",
        )(observed_hbm, *keep_vmem(*operands))

    turned = keep_vmem(
        pl.pallas_call(
            turn_kernel, out_shape=pltpu.VMEM((w, rows), bf16), in_specs=[in_vmem] * 2, out_specs=in_vmem,
            compiler_params=params, cost_estimate=price(0), name="turn"
        )(left, *keep_vmem(error))
    )
    grad_sum, *following = gradient(0, *held)
    parts = [None] * count
    for s in range(1, steps):
        held = []
        for i in range(count):
            right, = keep_vmem(moving[i])
            if s + 1 == steps and i + 1 == count:
                grad_in, = keep_vmem(grad_sum)
                error, theirs, mine = pl.pallas_call(
                    functools.partial(last_kernel, s, *spans[i], scale),
                    out_shape=[tiles[i], pltpu.VMEM((rows // 2, w), bf16), pltpu.VMEM((rows // 2, w), f32)],
                    in_specs=[in_vmem] * 8,
                    out_specs=[in_vmem] * 3,
                    input_output_aliases={3: 0},
                    compiler_params=params,
                    cost_estimate=price(s),
                    name="last_visit",
                )(right, left, turned[0], *keep_vmem(following[i]), codes, shifts, *keep_vmem(error), grad_in)
                continue
            if s + 1 < steps:
                parts[i], error = visit(s, i, moving[i], following[i], error)
            else:
                right_out, error = pl.pallas_call(
                    functools.partial(settle_kernel, s, *spans[i], scale),
                    out_shape=[pltpu.HBM(right_factor.shape, bf16), tiles[i]],
                    in_specs=[in_vmem] * 7,
                    out_specs=[in_hbm, in_vmem],
                    scratch_shapes=[parts_of[i], pltpu.SemaphoreType.DMA],
                    input_output_aliases={3: 1},
                    compiler_params=params,
                    cost_estimate=price(s),
                    name="settle",
                )(right, left, turned[0], *keep_vmem(following[i]), codes, shifts, *keep_vmem(error))
            held += [error, moving[i]]
            if s + 1 < steps:
                moving[i] = passed_along(parts[i])
            else:
                grad_sum = grad_sum + lax.dot_general(
                    error, held[-1], (((0,), (0,)), ((), ())), preferred_element_type=f32
                )
        if s + 1 < steps:
            grad_sum, *following = gradient(s, *held, grad_sum)

    half = pltpu.VMEM((rows // 2, w), bf16)
    chip_sum = pl.pallas_call(
        combine_kernel, out_shape=half, in_specs=[in_vmem] * 2, out_specs=in_vmem, compiler_params=params, name="combine"
    )(*keep_vmem(mine, both(theirs, 1)))
    renewed = pl.pallas_call(
        functools.partial(renew_kernel, scale), out_shape=half, in_specs=[in_vmem] * 2, out_specs=in_vmem,
        compiler_params=params, name="renew"
    )(*keep_vmem(both(chip_sum, 2)), left)
    new_left = both(renewed, 1).reshape(rows, w)
    return tuple(
        pl.pallas_call(
            functools.partial(store_kernel, spans[-1][0], scale),
            out_shape=[jax.ShapeDtypeStruct((rows, w), bf16), jax.ShapeDtypeStruct(right_factor.shape, bf16)],
            in_specs=[in_vmem] * 4 + [in_hbm],
            out_specs=[in_hbm] * 2,
            scratch_shapes=[parts_of[-1], pltpu.SemaphoreType.DMA((2,))],
            input_output_aliases={4: 1},
            compiler_params=params,
            name="store",
        )(*keep_vmem(new_left, moving[-1], error), left, *keep_hbm(right_out))
    )


def solution(mesh):
    in_specs = (
        P("blk", None),
        P("lane", "blk", None),
        P("lane", None, None, "blk"),
        P("blk"),
        P("lane", None, "blk"),
    )
    out_specs = (P("blk", None), P("lane", "blk", None))
    return jax.shard_map(local, mesh=mesh, in_specs=in_specs, out_specs=out_specs, check_vma=False)
```

```python
import functools
import math

import jax
import jax.numpy as jnp
from jax import lax
from jax.experimental import pallas as pl
from jax.experimental.pallas import tpu as pltpu
from jax.sharding import PartitionSpec as P

step_right = 0.25
step_left = 0.1
f32 = jnp.float32
bf16 = jnp.bfloat16
vmem_bytes = 12 << 20
chunk_rows = (256, 256)
in_vmem = pl.BlockSpec(memory_space=pltpu.VMEM)
in_hbm = pl.BlockSpec(memory_space=pltpu.HBM)
costs = (1, 1, 1, 1)


def price(s):
    return pl.CostEstimate(flops=int(costs[s] * 2e8), bytes_accessed=int(costs[s] * 1e6), transcendentals=0)


params = pltpu.CompilerParams(vmem_limit_bytes=vmem_bytes)


def passed_along(value):
    count = lax.axis_size("blk")
    return lax.ppermute(value, "blk", [(i, (i + 1) % count) for i in range(count)])


def both(value, bit):
    groups = [[i, i ^ bit] for i in range(lax.axis_size("lane")) if i < i ^ bit]
    return lax.all_gather(value, "lane", axis=0, axis_index_groups=groups, tiled=False)


def keep_hbm(*arrays):
    return [pltpu.with_memory_space_constraint(x, pltpu.HBM) for x in arrays]


def keep_vmem(*arrays):
    return [pltpu.with_memory_space_constraint(x, pltpu.VMEM) for x in arrays]


def times_transposed(a, left):
    return lax.dot_general(a, left, (((1,), (1,)), ((), ())), preferred_element_type=f32)


def errors(predicted, target, codes, shifts, scale):
    rows, columns = predicted.shape
    by_row = jnp.broadcast_to(shifts, (128, rows)).T
    by_row = jnp.concatenate([by_row] * (columns // 128), axis=1)
    bits = jnp.right_shift(jnp.broadcast_to(codes, (rows, columns)), by_row) & 1
    return jnp.where(bits == 1, predicted * scale - target.astype(f32), 0.0).astype(bf16)


def stepped(right, error, left, scale):
    grad = jnp.dot(error, left, preferred_element_type=f32)
    return (right.astype(f32) - step_right * scale * grad).astype(bf16)


def first_kernel(spans, scale, right_hbm, left_hbm, observed_hbm, codes_hbm, shifts_hbm, out, error, left, codes, shifts, *refs):
    count = len(spans)
    rights, others, target, sems = refs[:count], refs[count : 2 * count - 1], refs[-2], refs[-1]
    pairs = [
        (right_hbm.at[0, pl.ds(*spans[0])], rights[0]),
        (left_hbm, left),
        (observed_hbm.at[0, 0, pl.ds(*spans[0])], target),
        (codes_hbm, codes),
        (shifts_hbm, shifts),
    ]
    for i in range(1, count):
        pairs.append((right_hbm.at[0, pl.ds(*spans[i])], rights[i]))
        pairs.append((observed_hbm.at[0, 0, pl.ds(*spans[i])], others[i - 1]))
    copies = [pltpu.make_async_copy(a, b, sems.at[i]) for i, (a, b) in enumerate(pairs)]
    for c in copies:
        c.start()
    for c in copies[:2]:
        c.wait()
    right = rights[0][...]
    predicted = times_transposed(right, left[...])
    for c in copies[2:5]:
        c.wait()
    err = errors(predicted, target[...], codes[...], shifts[0:1, 0, 0 : spans[0][1]], scale)
    error[...] = err
    out[...] = stepped(right, err, left[...], scale)
    for c in copies[5:]:
        c.wait()


def visit_kernel(s, a, n, scale, right, left, turned, target, codes, shifts, prior, out, error):
    predicted = times_transposed(right[...], left[...]) if s == 0 else jnp.dot(
        right[...], turned[...], preferred_element_type=f32
    )
    err = errors(predicted, target[...], codes[...], shifts[0:1, s, a : a + n], scale)
    error[...] = err
    out[...] = stepped(right[...], err, left[...], scale)


def gradient_kernel(s, spans, observed_hbm, *refs):
    count = len(spans)
    errors_rights, rest = refs[: 2 * count], refs[2 * count :]
    before, out, following, sems = rest[: -count - 2], rest[-count - 2], rest[-count - 1 : -1], rest[-1]
    copies = [
        pltpu.make_async_copy(observed_hbm.at[0, s + 1, pl.ds(*spans[i])], ref, sems.at[i])
        for i, ref in enumerate(following)
    ]
    for c in copies:
        c.start()
    total = before[0][...] if before else None
    for i in range(count):
        error, right = errors_rights[2 * i : 2 * i + 2]
        term = lax.dot_general(error[...], right[...], (((0,), (0,)), ((), ())), preferred_element_type=f32)
        total = term if total is None else total + term
    out[...] = total
    for c in copies:
        c.wait()


def turn_kernel(left, prior, out):
    out[...] = left[...].T


def last_kernel(s, a, n, scale, right, left, turned, target, codes, shifts, prior, grad_sum, out, theirs, mine, error):
    half = left.shape[0] // 2
    core = lax.rem(lax.axis_index("lane"), 2)
    predicted = jnp.dot(right[...], turned[...], preferred_element_type=f32)
    err = errors(predicted, target[...], codes[...], shifts[0:1, s, a : a + n], scale)
    error[...] = err
    for ref, which in ((theirs, 1 - core), (mine, core)):
        own = pl.ds(pl.multiple_of(which * half, half), half)
        term = lax.dot_general(
            error[:, own], right[...], (((0,), (0,)), ((), ())), preferred_element_type=f32
        )
        ref[...] = (grad_sum[own, :] + term).astype(ref.dtype)
    out[...] = stepped(right[...], err, left[...], scale)


def settle_kernel(s, a, n, scale, right, left, turned, target, codes, shifts, prior, right_out, error, fresh, sem):
    visit_kernel(s, a, n, scale, right, left, turned, target, codes, shifts, prior, fresh, error)
    copy = pltpu.make_async_copy(fresh, right_out.at[0, pl.ds(a, n)], sem)
    copy.start()
    copy.wait()


def combine_kernel(mine, sent, out):
    core = lax.rem(lax.axis_index("lane"), 2)
    out[...] = (mine[...] + sent[1 - core].astype(f32)).astype(bf16)


def renew_kernel(scale, sums, left, out):
    half = out.shape[0]
    core = lax.rem(lax.axis_index("lane"), 2)
    own = left[pl.ds(pl.multiple_of(core * half, half), half), :].astype(f32)
    total = sums[0].astype(f32) + sums[1].astype(f32)
    out[...] = (own - step_left * scale * total).astype(bf16)


def store_kernel(first, left, part, right_hbm, left_hbm, right_out, sems):
    pairs = [(left, left_hbm), (part, right_out.at[0, pl.ds(first, part.shape[0])])]
    copies = [pltpu.make_async_copy(a, b, sems.at[i]) for i, (a, b) in enumerate(pairs)]
    for c in copies:
        c.start()
    for c in copies:
        c.wait()


def local(left_factor, right_factor, observed, row_codes, shift_codes):
    rows, w = left_factor.shape
    scale = 1.0 / math.sqrt(w)
    steps = observed.shape[1]
    spans = [(sum(chunk_rows[:i]), n) for i, n in enumerate(chunk_rows)]
    count = len(spans)
    parts_of = [pltpu.VMEM((n, w), bf16) for _, n in spans]
    tiles = [pltpu.VMEM((n, rows), bf16) for _, n in spans]
    right_hbm, left_hbm, observed_hbm, codes_hbm, shifts_hbm = keep_hbm(
        right_factor, left_factor, observed, row_codes[None, :], shift_codes
    )
    after, error, plain_left, codes, shifts, *loaded = pl.pallas_call(
        functools.partial(first_kernel, spans, scale),
        out_shape=[parts_of[0], tiles[0], pltpu.VMEM((rows, w), bf16), pltpu.VMEM((1, rows), jnp.int32),
                   pltpu.VMEM(shift_codes.shape, jnp.int32), *parts_of, *tiles[1:]],
        in_specs=[in_hbm] * 5,
        out_specs=[in_vmem] * (2 * count + 4),
        scratch_shapes=[tiles[0], pltpu.SemaphoreType.DMA((2 * count + 3,))],
        compiler_params=params,
        cost_estimate=price(0),
        name="first_visit",
    )(right_hbm, left_hbm, observed_hbm, codes_hbm, shifts_hbm)
    left, codes, shifts = keep_vmem(plain_left, codes, shifts)

    def visit(s, i, right, target, prior):
        right, target, prior = keep_vmem(right, target, prior)
        return pl.pallas_call(
            functools.partial(visit_kernel, s, *spans[i], scale),
            out_shape=[parts_of[i], tiles[i]],
            in_specs=[in_vmem] * 7,
            out_specs=[in_vmem] * 2,
            input_output_aliases={3: 1},
            compiler_params=params,
            cost_estimate=price(s),
            name="visit",
        )(right, left, turned[0], target, codes, shifts, prior)

    turned = [left]
    moving, held = [passed_along(after)], [error, loaded[0]]
    turned = keep_vmem(
        pl.pallas_call(
            turn_kernel, out_shape=pltpu.VMEM((w, rows), bf16), in_specs=[in_vmem] * 2, out_specs=in_vmem,
            compiler_params=params, cost_estimate=price(0), name="turn"
        )(left, *keep_vmem(error))
    )
    for i in range(1, count):
        after, error = visit(0, i, loaded[i], loaded[count + i - 1], turned[0])
        moving.append(passed_along(after))
        held += [error, loaded[i]]

    def gradient(s, *operands):
        added = len(operands) > 2 * count
        return pl.pallas_call(
            functools.partial(gradient_kernel, s, spans),
            out_shape=[pltpu.VMEM((rows, w), f32), *tiles],
            in_specs=[in_hbm] + [in_vmem] * len(operands),
            out_specs=[in_vmem] * (count + 1),
            scratch_shapes=[pltpu.SemaphoreType.DMA((count,))],
            input_output_aliases={2 * count + 1: 0} if added else {},
            compiler_params=params,
            cost_estimate=price(s),
            name="gradient",
        )(observed_hbm, *keep_vmem(*operands))

    grad_sum, *following = gradient(0, *held)
    parts = [None] * count
    for s in range(1, steps):
        held = []
        for i in range(count):
            right, = keep_vmem(moving[i])
            if s + 1 == steps and i + 1 == count:
                grad_in, = keep_vmem(grad_sum)
                parts[i], theirs, mine = pl.pallas_call(
                    functools.partial(last_kernel, s, *spans[i], scale),
                    out_shape=[parts_of[i], pltpu.VMEM((rows // 2, w), bf16), pltpu.VMEM((rows // 2, w), f32)],
                    in_specs=[in_vmem] * 8,
                    out_specs=[in_vmem] * 3,
                    scratch_shapes=[tiles[i]],
                    compiler_params=params,
                    cost_estimate=price(s),
                    name="last_visit",
                )(right, left, turned[0], *keep_vmem(following[i]), codes, shifts, *keep_vmem(error), grad_in)
                continue
            if s + 1 < steps:
                parts[i], error = visit(s, i, moving[i], following[i], error)
            else:
                right_out, error = pl.pallas_call(
                    functools.partial(settle_kernel, s, *spans[i], scale),
                    out_shape=[pltpu.HBM(right_factor.shape, bf16), tiles[i]],
                    in_specs=[in_vmem] * 7,
                    out_specs=[in_hbm, in_vmem],
                    scratch_shapes=[parts_of[i], pltpu.SemaphoreType.DMA],
                    input_output_aliases={3: 1},
                    compiler_params=params,
                    cost_estimate=price(s),
                    name="settle",
                )(right, left, turned[0], *keep_vmem(following[i]), codes, shifts, *keep_vmem(error))
            held += [error, moving[i]]
            if s + 1 < steps:
                moving[i] = passed_along(parts[i])
            else:
                grad_sum = grad_sum + lax.dot_general(
                    error, held[-1], (((0,), (0,)), ((), ())), preferred_element_type=f32
                )
        if s + 1 < steps:
            grad_sum, *following = gradient(s, *held, grad_sum)

    half = pltpu.VMEM((rows // 2, w), bf16)
    chip_sum = pl.pallas_call(
        combine_kernel, out_shape=half, in_specs=[in_vmem] * 2, out_specs=in_vmem, compiler_params=params, name="combine"
    )(*keep_vmem(mine, both(theirs, 1)))
    renewed = pl.pallas_call(
        functools.partial(renew_kernel, scale), out_shape=half, in_specs=[in_vmem] * 2, out_specs=in_vmem,
        compiler_params=params, name="renew"
    )(*keep_vmem(both(chip_sum, 2)), left)
    new_left = both(renewed, 1).reshape(rows, w)
    return tuple(
        pl.pallas_call(
            functools.partial(store_kernel, spans[-1][0]),
            out_shape=[jax.ShapeDtypeStruct((rows, w), bf16), jax.ShapeDtypeStruct(right_factor.shape, bf16)],
            in_specs=[in_vmem] * 2 + [in_hbm],
            out_specs=[in_hbm] * 2,
            scratch_shapes=[pltpu.SemaphoreType.DMA((2,))],
            input_output_aliases={2: 1},
            compiler_params=params,
            name="store",
        )(*keep_vmem(new_left, parts[-1]), *keep_hbm(right_out))
    )


def solution(mesh):
    in_specs = (
        P("blk", None),
        P("lane", "blk", None),
        P("lane", None, None, "blk"),
        P("blk"),
        P("lane", None, "blk"),
    )
    out_specs = (P("blk", None), P("lane", "blk", None))
    return jax.shard_map(local, mesh=mesh, in_specs=in_specs, out_specs=out_specs, check_vma=False)
```

```python
import functools
import math

import jax
import jax.numpy as jnp
from jax import lax
from jax.experimental import pallas as pl
from jax.experimental.pallas import tpu as pltpu
from jax.sharding import PartitionSpec as P

step_right = 0.25
step_left = 0.1
f32 = jnp.float32
bf16 = jnp.bfloat16
vmem_bytes = 12 << 20
chunk_rows = (256, 256)
in_vmem = pl.BlockSpec(memory_space=pltpu.VMEM)
in_hbm = pl.BlockSpec(memory_space=pltpu.HBM)
costs = (1, 1, 1, 1)


def price(s):
    return pl.CostEstimate(flops=int(costs[s] * 2e8), bytes_accessed=int(costs[s] * 1e6), transcendentals=0)


params = pltpu.CompilerParams(vmem_limit_bytes=vmem_bytes)


def passed_along(value):
    count = lax.axis_size("blk")
    return lax.ppermute(value, "blk", [(i, (i + 1) % count) for i in range(count)])


def both(value, bit):
    groups = [[i, i ^ bit] for i in range(lax.axis_size("lane")) if i < i ^ bit]
    return lax.all_gather(value, "lane", axis=0, axis_index_groups=groups, tiled=False)


def keep_hbm(*arrays):
    return [pltpu.with_memory_space_constraint(x, pltpu.HBM) for x in arrays]


def keep_vmem(*arrays):
    return [pltpu.with_memory_space_constraint(x, pltpu.VMEM) for x in arrays]


def times_transposed(a, left):
    return lax.dot_general(a, left, (((1,), (1,)), ((), ())), preferred_element_type=f32)


def errors(predicted, target, codes, shifts, scale):
    rows, columns = predicted.shape
    by_row = jnp.broadcast_to(shifts, (128, rows)).T
    by_row = jnp.concatenate([by_row] * (columns // 128), axis=1)
    bits = jnp.right_shift(jnp.broadcast_to(codes, (rows, columns)), by_row) & 1
    return jnp.where(bits == 1, predicted * scale - target.astype(f32), 0.0).astype(bf16)


def stepped(right, error, left, scale):
    grad = jnp.dot(error, left, preferred_element_type=f32)
    return (right.astype(f32) - step_right * scale * grad).astype(bf16)


def first_kernel(spans, scale, right_hbm, left_hbm, observed_hbm, codes_hbm, shifts_hbm, out, error, left, codes, shifts, *refs):
    count = len(spans)
    rights, others, target, sems = refs[:count], refs[count : 2 * count - 1], refs[-2], refs[-1]
    half = left.shape[0] // 2
    pairs = [
        (right_hbm.at[0, pl.ds(*spans[0])], rights[0]),
        (left_hbm.at[pl.ds(0, half)], left.at[pl.ds(0, half)]),
        (observed_hbm.at[0, 0, pl.ds(*spans[0])], target),
        (codes_hbm, codes),
        (shifts_hbm, shifts),
        (left_hbm.at[pl.ds(half, half)], left.at[pl.ds(half, half)]),
    ]
    for i in range(1, count):
        pairs.append((right_hbm.at[0, pl.ds(*spans[i])], rights[i]))
        pairs.append((observed_hbm.at[0, 0, pl.ds(*spans[i])], others[i - 1]))
    copies = [pltpu.make_async_copy(a, b, sems.at[i]) for i, (a, b) in enumerate(pairs)]
    for c in copies:
        c.start()
    grad = None
    copies[0].wait()
    for i in range(2):
        own = slice(i * half, (i + 1) * half)
        copies[1 + 4 * i].wait()
        predicted = times_transposed(rights[0][...], left[own, :])
        if i == 0:
            for c in copies[2:5]:
                c.wait()
        err = errors(predicted, target[:, own], codes[:, own], shifts[0:1, 0, 0 : spans[0][1]], scale)
        error[:, own] = err
        term = jnp.dot(err, left[own, :], preferred_element_type=f32)
        grad = term if grad is None else grad + term
    out[...] = (rights[0][...].astype(f32) - step_right * scale * grad).astype(bf16)
    for c in copies[6:]:
        c.wait()


def visit_kernel(s, a, n, scale, right, left, target, codes, shifts, prior, out, error):
    predicted = times_transposed(right[...], left[...])
    err = errors(predicted, target[...], codes[...], shifts[0:1, s, a : a + n], scale)
    error[...] = err
    out[...] = stepped(right[...], err, left[...], scale)


def gradient_kernel(s, spans, observed_hbm, *refs):
    count = len(spans)
    errors_rights, rest = refs[: 2 * count], refs[2 * count :]
    before, out, following, sems = rest[: -count - 2], rest[-count - 2], rest[-count - 1 : -1], rest[-1]
    copies = [
        pltpu.make_async_copy(observed_hbm.at[0, s + 1, pl.ds(*spans[i])], ref, sems.at[i])
        for i, ref in enumerate(following)
    ]
    for c in copies:
        c.start()
    total = before[0][...] if before else None
    for i in range(count):
        error, right = errors_rights[2 * i : 2 * i + 2]
        term = lax.dot_general(error[...], right[...], (((0,), (0,)), ((), ())), preferred_element_type=f32)
        total = term if total is None else total + term
    out[...] = total
    for c in copies:
        c.wait()


def last_kernel(s, a, n, scale, right, left, target, codes, shifts, prior, grad_sum, out, theirs, mine, error):
    half = left.shape[0] // 2
    core = lax.rem(lax.axis_index("lane"), 2)
    predicted = times_transposed(right[...], left[...])
    err = errors(predicted, target[...], codes[...], shifts[0:1, s, a : a + n], scale)
    error[...] = err
    for ref, which in ((theirs, 1 - core), (mine, core)):
        own = pl.ds(pl.multiple_of(which * half, half), half)
        term = lax.dot_general(
            error[:, own], right[...], (((0,), (0,)), ((), ())), preferred_element_type=f32
        )
        ref[...] = (grad_sum[own, :] + term).astype(ref.dtype)
    out[...] = stepped(right[...], err, left[...], scale)


def settle_kernel(s, a, n, scale, right, left, target, codes, shifts, prior, right_out, error, fresh, sem):
    visit_kernel(s, a, n, scale, right, left, target, codes, shifts, prior, fresh, error)
    copy = pltpu.make_async_copy(fresh, right_out.at[0, pl.ds(a, n)], sem)
    copy.start()
    copy.wait()


def combine_kernel(mine, sent, out):
    core = lax.rem(lax.axis_index("lane"), 2)
    out[...] = (mine[...] + sent[1 - core].astype(f32)).astype(bf16)


def renew_kernel(scale, sums, left, out):
    half = out.shape[0]
    core = lax.rem(lax.axis_index("lane"), 2)
    own = left[pl.ds(pl.multiple_of(core * half, half), half), :].astype(f32)
    total = sums[0].astype(f32) + sums[1].astype(f32)
    out[...] = (own - step_left * scale * total).astype(bf16)


def store_kernel(first, left, part, right_hbm, left_hbm, right_out, sems):
    pairs = [(left, left_hbm), (part, right_out.at[0, pl.ds(first, part.shape[0])])]
    copies = [pltpu.make_async_copy(a, b, sems.at[i]) for i, (a, b) in enumerate(pairs)]
    for c in copies:
        c.start()
    for c in copies:
        c.wait()


def local(left_factor, right_factor, observed, row_codes, shift_codes):
    rows, w = left_factor.shape
    scale = 1.0 / math.sqrt(w)
    steps = observed.shape[1]
    spans = [(sum(chunk_rows[:i]), n) for i, n in enumerate(chunk_rows)]
    count = len(spans)
    parts_of = [pltpu.VMEM((n, w), bf16) for _, n in spans]
    tiles = [pltpu.VMEM((n, rows), bf16) for _, n in spans]
    right_hbm, left_hbm, observed_hbm, codes_hbm, shifts_hbm = keep_hbm(
        right_factor, left_factor, observed, row_codes[None, :], shift_codes
    )
    after, error, plain_left, codes, shifts, *loaded = pl.pallas_call(
        functools.partial(first_kernel, spans, scale),
        out_shape=[parts_of[0], tiles[0], pltpu.VMEM((rows, w), bf16), pltpu.VMEM((1, rows), jnp.int32),
                   pltpu.VMEM(shift_codes.shape, jnp.int32), *parts_of, *tiles[1:]],
        in_specs=[in_hbm] * 5,
        out_specs=[in_vmem] * (2 * count + 4),
        scratch_shapes=[tiles[0], pltpu.SemaphoreType.DMA((2 * count + 4,))],
        compiler_params=params,
        cost_estimate=price(0),
        name="first_visit",
    )(right_hbm, left_hbm, observed_hbm, codes_hbm, shifts_hbm)
    left, codes, shifts = keep_vmem(plain_left, codes, shifts)

    def visit(s, i, right, target, prior):
        right, target, prior = keep_vmem(right, target, prior)
        return pl.pallas_call(
            functools.partial(visit_kernel, s, *spans[i], scale),
            out_shape=[parts_of[i], tiles[i]],
            in_specs=[in_vmem] * 6,
            out_specs=[in_vmem] * 2,
            input_output_aliases={2: 1},
            compiler_params=params,
            cost_estimate=price(s),
            name="visit",
        )(right, left, target, codes, shifts, prior)

    moving, held = [passed_along(after)], [error, loaded[0]]
    for i in range(1, count):
        after, error = visit(0, i, loaded[i], loaded[count + i - 1], error)
        moving.append(passed_along(after))
        held += [error, loaded[i]]

    def gradient(s, *operands):
        added = len(operands) > 2 * count
        return pl.pallas_call(
            functools.partial(gradient_kernel, s, spans),
            out_shape=[pltpu.VMEM((rows, w), f32), *tiles],
            in_specs=[in_hbm] + [in_vmem] * len(operands),
            out_specs=[in_vmem] * (count + 1),
            scratch_shapes=[pltpu.SemaphoreType.DMA((count,))],
            input_output_aliases={2 * count + 1: 0} if added else {},
            compiler_params=params,
            cost_estimate=price(s),
            name="gradient",
        )(observed_hbm, *keep_vmem(*operands))

    grad_sum, *following = gradient(0, *held)
    parts = [None] * count
    for s in range(1, steps):
        held = []
        for i in range(count):
            right, = keep_vmem(moving[i])
            if s + 1 == steps and i + 1 == count:
                grad_in, = keep_vmem(grad_sum)
                parts[i], theirs, mine = pl.pallas_call(
                    functools.partial(last_kernel, s, *spans[i], scale),
                    out_shape=[parts_of[i], pltpu.VMEM((rows // 2, w), bf16), pltpu.VMEM((rows // 2, w), f32)],
                    in_specs=[in_vmem] * 7,
                    out_specs=[in_vmem] * 3,
                    scratch_shapes=[tiles[i]],
                    compiler_params=params,
                    cost_estimate=price(s),
                    name="last_visit",
                )(right, left, *keep_vmem(following[i]), codes, shifts, *keep_vmem(error), grad_in)
                continue
            if s + 1 < steps:
                parts[i], error = visit(s, i, moving[i], following[i], error)
            else:
                right_out, error = pl.pallas_call(
                    functools.partial(settle_kernel, s, *spans[i], scale),
                    out_shape=[pltpu.HBM(right_factor.shape, bf16), tiles[i]],
                    in_specs=[in_vmem] * 6,
                    out_specs=[in_hbm, in_vmem],
                    scratch_shapes=[parts_of[i], pltpu.SemaphoreType.DMA],
                    input_output_aliases={2: 1},
                    compiler_params=params,
                    cost_estimate=price(s),
                    name="settle",
                )(right, left, *keep_vmem(following[i]), codes, shifts, *keep_vmem(error))
            held += [error, moving[i]]
            if s + 1 < steps:
                moving[i] = passed_along(parts[i])
            else:
                grad_sum = grad_sum + lax.dot_general(
                    error, held[-1], (((0,), (0,)), ((), ())), preferred_element_type=f32
                )
        if s + 1 < steps:
            grad_sum, *following = gradient(s, *held, grad_sum)

    half = pltpu.VMEM((rows // 2, w), bf16)
    chip_sum = pl.pallas_call(
        combine_kernel, out_shape=half, in_specs=[in_vmem] * 2, out_specs=in_vmem, compiler_params=params, name="combine"
    )(*keep_vmem(mine, both(theirs, 1)))
    renewed = pl.pallas_call(
        functools.partial(renew_kernel, scale), out_shape=half, in_specs=[in_vmem] * 2, out_specs=in_vmem,
        compiler_params=params, name="renew"
    )(*keep_vmem(both(chip_sum, 2)), left)
    new_left = both(renewed, 1).reshape(rows, w)
    return tuple(
        pl.pallas_call(
            functools.partial(store_kernel, spans[-1][0]),
            out_shape=[jax.ShapeDtypeStruct((rows, w), bf16), jax.ShapeDtypeStruct(right_factor.shape, bf16)],
            in_specs=[in_vmem] * 2 + [in_hbm],
            out_specs=[in_hbm] * 2,
            scratch_shapes=[pltpu.SemaphoreType.DMA((2,))],
            input_output_aliases={2: 1},
            compiler_params=params,
            name="store",
        )(*keep_vmem(new_left, parts[-1]), *keep_hbm(right_out))
    )


def solution(mesh):
    in_specs = (
        P("blk", None),
        P("lane", "blk", None),
        P("lane", None, None, "blk"),
        P("blk"),
        P("lane", None, "blk"),
    )
    out_specs = (P("blk", None), P("lane", "blk", None))
    return jax.shard_map(local, mesh=mesh, in_specs=in_specs, out_specs=out_specs, check_vma=False)
```
